256 devices in a mesh: expert: 16 (over y, x), dp: 8 (over z), tensor: 2 (over core).
Axes of the slice: x: 4, y: 4, z: 8, core: 2. Of those that a mesh axis runs over, the one named last changes fastest.
Arguments:
- grad_out: bfloat16 [16384, 7168], P(('expert', 'dp'), 'tensor'), may hold values from -6 to 6
- route_weight: float32 [16384, 8], P(('expert', 'dp')), may hold values from 0.02 to 0.5
- expert_ids: int32 [16384, 8], P(('expert', 'dp')), may hold values from 0 to 15, as said below
- hidden: bfloat16 [16, 8, 16, 96, 1024], P('expert', 'dp', None, None, 'tensor'), may hold values from -6 to 6
- weight: bfloat16 [16, 7168, 1024], P('expert', 'dp', 'tensor'), may hold values from -0.1875 to 0.1875
- moment: bfloat16 [16, 7168, 1024], P('expert', 'dp', 'tensor'), may hold values from -6 to 6
- second: bfloat16 [16, 7168, 1024], P('expert', 'dp', 'tensor'), may hold values from 0.099609375 to 2
- mlp_in: float32 [32, 5], replicated, may hold values from -2.5 to 2.5
- mlp_bias: float32 [32], replicated, may hold values from -3 to 3
- mlp_out: float32 [2, 32], replicated, may hold values from -1 to 1
Outputs:
- update: bfloat16 [16, 7168, 1024], P('expert', 'dp', 'tensor')
- moment_out: bfloat16 [16, 7168, 1024], P('expert', 'dp', 'tensor')
- second_out: bfloat16 [16, 7168, 1024], P('expert', 'dp', 'tensor')
The draws below stay inside these ranges and needn't reach their ends.
Inputs may be any that keep to these rules, and one draw needn't show every extreme that they name: `expert_ids`: each token names 8 different experts. Among the 128 tokens of one block no expert is named more than 96 times. For each dp index, one expert is named exactly 96 times in every block of that dp index.
All inputs are finite; a program needn't handle non-finite values.
Results may differ from the reference program's by a relative error of at most 0.013.
Values may be sent and summed in bfloat16 or wider, within the bound.
No kernel may reach another device: no remote copies, remote signals or barrier semaphores. Data moves between devices by JAX's collectives and lax.ppermute only.
A program may use at most 192 MiB of HBM per device.

```python
import math
import jax
import jax.numpy as jnp
from jax import lax

D = 7168
HW = 1024
TOK_DEV = 128
MLP_HID = 32
FEAT = 5
EXPERTS = 16
TOP = 8
CAP = 96
TOKENS = 16384
N_EXPERT = 16
N_DP = 8


def draw_expert_ids(key, part):
    key = jax.random.fold_in(key, 11)
    block_total = TOKENS // TOK_DEV
    average = TOK_DEV * TOP // EXPERTS
    surplus = CAP - average
    chosen = jax.random.randint(jax.random.fold_in(key, 7), (N_DP,), 0, EXPERTS)

    def one_block(block_index):
        block_key = jax.random.fold_in(key, block_index + 100)
        key_perm, key_offsets, key_tokens, key_slots = jax.random.split(block_key, 4)
        target = chosen[block_index % N_DP]
        scores = jax.random.permutation(key_perm, EXPERTS)
        scores = jnp.where(jnp.arange(EXPERTS) == target, -1, scores)
        ranking = jnp.argsort(scores)
        offsets = jax.random.randint(key_offsets, (EXPERTS // 2,), 0, surplus + 1)
        offsets = offsets.at[0].set(surplus)
        loads = jnp.stack([average + offsets, average - offsets], axis=1).reshape(EXPERTS)
        counts = jnp.zeros((EXPERTS,), jnp.int32).at[ranking].set(loads.astype(jnp.int32))
        bounds = jnp.cumsum(counts)
        position = jnp.arange(TOP * TOK_DEV)
        sequence = jnp.sum((position[:, None] >= bounds[None, :]).astype(jnp.int32), axis=1)
        layout = sequence.reshape(TOP, TOK_DEV).T
        layout = layout[jax.random.permutation(key_tokens, TOK_DEV)]
        shuffle_keys = jax.random.randint(key_slots, (TOK_DEV, TOP), 0, 1 << 20) * TOP + jnp.arange(TOP)
        return jnp.take_along_axis(layout, jnp.argsort(shuffle_keys, axis=1), axis=1)
    result = jax.lax.map(one_block, jnp.arange(block_total))
    return result.reshape(TOKENS, TOP).astype(jnp.int32)


def block_levels(stream_key, extent, cuts, low, top_value):
    def one(axis_at, shards_of):
        heights = jax.random.uniform(jax.random.fold_in(jax.random.fold_in(stream_key, 6), axis_at), (shards_of,), jnp.float32, low / len(cuts), top_value / len(cuts))
        return jnp.repeat(jnp.exp(heights), extent[axis_at] // shards_of).reshape((-1,) + (1,) * (len(extent) - axis_at - 1))

    loudness = one(*cuts[0])
    for cut in cuts[1:]:
        loudness = loudness * one(*cut)
    return loudness


def gaussian(stream_key, dims, spread, bound, shards=(), held_as=jnp.bfloat16):
    drawn = jax.random.normal(stream_key, dims, jnp.float32) * spread
    if len(shards) > 0:
        drawn = block_levels(stream_key, dims, shards, -0.22, 0.18) * drawn
    return jnp.clip(drawn, min=-bound, max=bound).astype(held_as)


def setup_inputs(seed: int = 0) -> dict:
    seeds = jax.random.split(jax.random.key(seed), 11)
    grad_out = gaussian(seeds[0], (TOKENS, D), 1.0, 6.0, ((0, 128), (1, 2)))
    route_weight = jnp.clip(jnp.exp(math.log(0.5) - 3.218876 * jax.random.uniform(seeds[1], (TOKENS, TOP), jnp.float32) ** block_levels(seeds[1], (TOKENS, TOP), ((0, 128),), -0.2, 0.2)), 0.02, 0.5)
    expert_ids = draw_expert_ids(jax.random.fold_in(seeds[10], 71), 0)
    hidden = gaussian(seeds[3], (EXPERTS, N_DP, N_EXPERT, CAP, HW), 1.0, 6.0, ((0, 16), (1, 8), (4, 2)))
    weight = gaussian(seeds[4], (EXPERTS, D, HW), HW ** -0.5, 0.1875, ((0, 16), (1, 8), (2, 2)))
    moment = gaussian(seeds[5], (EXPERTS, D, HW), 1.0, 6.0, ((0, 16), (1, 8), (2, 2)))
    second = jnp.clip(jnp.exp(math.log(2.0) - 2.9996462 * jax.random.uniform(seeds[6], (EXPERTS, D, HW), jnp.float32) ** block_levels(seeds[6], (EXPERTS, D, HW), ((0, 16), (1, 8), (2, 2)), -0.2, 0.2)), 0.099609375, 2.0).astype(jnp.bfloat16)
    mlp_in = gaussian(seeds[7], (MLP_HID, FEAT), FEAT ** -0.5, 2.5, (), jnp.float32)
    mlp_bias = gaussian(seeds[8], (MLP_HID,), 0.5, 3.0, (), jnp.float32)
    mlp_out = gaussian(seeds[9], (2, MLP_HID), MLP_HID ** -0.5, 1.0, (), jnp.float32)
    return dict(grad_out=grad_out, route_weight=route_weight, expert_ids=expert_ids, hidden=hidden, weight=weight, moment=moment, second=second, mlp_in=mlp_in, mlp_bias=mlp_bias, mlp_out=mlp_out)


LOSS_SCALE = 16.0
FIRST_DECAY = 0.9
SECOND_DECAY = 0.95
WEIGHT_FEATURE = 32.0
EPSILON = 1e-08

def slot_tables(expert_ids, route_weight, num_experts, capacity):
    token_total = expert_ids.shape[0]
    onehot = (expert_ids[:, :, None] == jnp.arange(num_experts, dtype=jnp.int32)).astype(jnp.int32)
    per_token = lax.optimization_barrier(jnp.sum(onehot, axis=1))
    before = jnp.cumsum(per_token, axis=0) - per_token
    slots = jnp.take_along_axis(before, expert_ids, axis=1).astype(jnp.int32)
    tokens = jnp.broadcast_to(jnp.arange(token_total, dtype=jnp.int32)[:, None], expert_ids.shape)
    token_index = jnp.zeros((num_experts, capacity), jnp.int32).at[expert_ids, slots].set(tokens)
    weight_sel = jnp.zeros((num_experts, capacity), jnp.float32).at[expert_ids, slots].set(route_weight)
    return (token_index, weight_sel, lax.optimization_barrier(jnp.sum(per_token, axis=0)))

def learned_update(grad_sum, weight, moment, second, mlp_in, mlp_bias, mlp_out):
    grad = grad_sum / LOSS_SCALE
    moment_new = FIRST_DECAY * moment.astype(jnp.float32) + (1.0 - FIRST_DECAY) * grad
    second_new = SECOND_DECAY * second.astype(jnp.float32) + (1.0 - SECOND_DECAY) * grad * grad
    inverse = lax.rsqrt(second_new + EPSILON)
    features = jnp.stack([grad, moment_new, grad * inverse, moment_new * inverse, WEIGHT_FEATURE * weight.astype(jnp.float32)])
    units = jax.nn.relu(jnp.einsum('jf,frc->jrc', mlp_in, features, precision=lax.Precision.HIGHEST) + mlp_bias[:, None, None])
    network = jnp.einsum('oj,jrc->orc', mlp_out, units, precision=lax.Precision.HIGHEST)
    step_out = network[0] * jnp.exp(jnp.tanh(network[1]))
    return (step_out.astype(jnp.bfloat16), moment_new.astype(jnp.bfloat16), second_new.astype(jnp.bfloat16))

def update_blocks(grad_sum, weight, moment, second, mlp_in, mlp_bias, mlp_out):
    row_total = grad_sum.shape[0]
    col_total = grad_sum.shape[1]
    block_rows = 128 if row_total % 128 == 0 else row_total
    block_count = row_total // block_rows

    def apply_block(pieces):
        return learned_update(pieces[0], pieces[1], pieces[2], pieces[3], mlp_in, mlp_bias, mlp_out)
    pieces = (grad_sum.reshape(block_count, block_rows, col_total), weight.reshape(block_count, block_rows, col_total), moment.reshape(block_count, block_rows, col_total), second.reshape(block_count, block_rows, col_total))
    step_out, moment_new, second_new = lax.map(apply_block, pieces)
    return (step_out.reshape(row_total, col_total), moment_new.reshape(row_total, col_total), second_new.reshape(row_total, col_total))

def reference(grad_out, route_weight, expert_ids, hidden, weight, moment, second, mlp_in, mlp_bias, mlp_out):
    block_ids = expert_ids.reshape(N_EXPERT, N_DP, TOK_DEV, TOP)
    block_weights = route_weight.reshape(N_EXPERT, N_DP, TOK_DEV, TOP)
    block_grads = grad_out.reshape(N_EXPERT, N_DP, TOK_DEV, D)

    def tables_of(ids_block, weights_block):
        token_index, weight_sel, per_expert = slot_tables(ids_block, weights_block, EXPERTS, CAP)
        return (token_index, weight_sel)
    token_index, weight_sel = jax.vmap(jax.vmap(tables_of))(block_ids, block_weights)
    source_range = jnp.arange(N_EXPERT, dtype=jnp.int32)[:, None]

    def expert_result(expert):

        def add_group(group, total):
            chosen_tokens = token_index[:, group, expert]
            chosen_weights = weight_sel[:, group, expert]
            source_grads = block_grads[:, group]
            gathered = source_grads[source_range, chosen_tokens].astype(jnp.float32)
            grad_rows = (chosen_weights[:, :, None] * gathered).astype(jnp.bfloat16).reshape(N_EXPERT * CAP, D)
            activations = hidden[expert, group].reshape(N_EXPERT * CAP, HW)
            partial_grad = lax.dot_general(grad_rows, activations, (((0,), (0,)), ((), ())), preferred_element_type=jnp.float32)
            rounded = lax.optimization_barrier(partial_grad.astype(jnp.bfloat16))
            return total + rounded.astype(jnp.float32)
        grad_sum = lax.fori_loop(0, N_DP, add_group, jnp.zeros((D, HW), jnp.float32))
        return update_blocks(grad_sum, weight[expert], moment[expert], second[expert], mlp_in, mlp_bias, mlp_out)
    update, moment_out, second_out = lax.map(expert_result, jnp.arange(EXPERTS, dtype=jnp.int32))
    return (update, moment_out, second_out)
```

```python
import functools

import jax
import jax.numpy as jnp
from jax import lax
from jax.experimental import pallas as pl
from jax.experimental.pallas import tpu as pltpu
from jax.sharding import PartitionSpec as P

BF = jnp.bfloat16
F32 = jnp.float32

LOSS_SCALE = 16.0
FIRST_DECAY = 0.9
SECOND_DECAY = 0.95
WEIGHT_FEATURE = 32.0
EPSILON = 1e-08

OFFSETS = (4, 3, -3, 2, -2, 1, -1, 0)
SIDE = 4
TABLE_ROWS = 32
MIB = 1 << 20


def along_x(k):
    return [(y * SIDE + x, y * SIDE + (x + k) % SIDE) for y in range(SIDE) for x in range(SIDE)]


def along_y(k):
    return [(y * SIDE + x, (y + k) % SIDE * SIDE + x) for y in range(SIDE) for x in range(SIDE)]


def mirrored(mask):
    return [(i, i ^ mask) for i in range(SIDE * SIDE)]


def ring_pair_gather(block_a, pairs_a, block_b, pairs_b):
    blocks = ((block_a, pairs_a), (block_b, pairs_b))
    near = []
    for block, pairs in blocks:
        near.append(lax.ppermute(block, "expert", pairs(1)))
        near.append(lax.ppermute(block, "expert", pairs(-1)))
    near = lax.optimization_barrier(tuple(near))
    far = []
    for k, (block, pairs) in enumerate(blocks):
        half = block.shape[0] // 2
        far.append(lax.ppermute(near[2 * k][:half], "expert", pairs(1)))
        far.append(lax.ppermute(near[2 * k + 1][half:], "expert", pairs(-1)))
    return [(block, near[2 * k], near[2 * k + 1], far[2 * k], far[2 * k + 1]) for k, (block, _) in enumerate(blocks)]


def torus_pair_gather(block_a, block_b):
    lines = ring_pair_gather(block_a, along_x, block_b, along_y)
    stacks = [
        jnp.stack([own, behind, ahead, jnp.concatenate([first, second], axis=0)])
        for own, behind, ahead, first, second in lines
    ]
    stacks = lax.optimization_barrier(tuple(stacks))
    return ring_pair_gather(stacks[0], along_y, stacks[1], along_x)


def piece_sources(expert, inner_is_x):
    y, x = expert // SIDE, expert % SIDE
    offsets = (0, -1, 1, 2)
    out = []
    for outer in offsets:
        for inner in offsets:
            dx, dy = (inner, outer) if inner_is_x else (outer, inner)
            out.append((y + dy) % SIDE * SIDE + (x + dx) % SIDE)
    return jnp.stack(out).astype(jnp.int32)


def gather_tables(table):
    for step in range(4):
        other = lax.ppermute(table, "expert", mirrored(1 << step))
        table = jnp.concatenate([table, other], axis=0)
    return table


def spread_kernel(capacity, meta, table, near, far, out):
    expert = meta[0]
    tokens = table.shape[-1]
    ids = table[0, 0:8, :].astype(F32)
    weight = table[0, 8:16, :].astype(F32) + table[0, 16:24, :].astype(F32)
    hit = (ids == expert.astype(F32)).astype(F32)
    named = jnp.sum(hit, axis=0, keepdims=True)
    scale = jnp.sum(hit * weight, axis=0, keepdims=True)
    earlier = (
        lax.broadcasted_iota(jnp.int32, (tokens, tokens), 0)
        < lax.broadcasted_iota(jnp.int32, (tokens, tokens), 1)
    ).astype(F32).astype(BF)
    slot = jnp.dot(
        jnp.broadcast_to(named, (16, tokens)).astype(BF), earlier, preferred_element_type=F32
    )[0:1, :]
    slot = jnp.where(named > 0.5, slot, -1.0)
    place = lax.broadcasted_iota(jnp.int32, (capacity, tokens), 0).astype(F32)
    chosen = jnp.where(place == slot, jnp.broadcast_to(scale, (capacity, tokens)), 0.0)
    high = chosen.astype(BF)
    low = (chosen - high.astype(F32)).astype(BF)
    left = jnp.concatenate([high, low], axis=0)
    width = near.shape[-1]
    core = meta[1]
    dims = (((0,), (0,)), ((), ()))
    mine = lax.dot_general(
        left, jnp.concatenate([near[0], near[0]], axis=0), dims, preferred_element_type=F32
    ).astype(BF)
    other = lax.dot_general(
        left, jnp.concatenate([far[0], far[0]], axis=0), dims, preferred_element_type=F32
    ).astype(BF)
    out[0, :, pl.ds(0, width)] = jnp.where(core == 0, mine, other)
    out[0, :, pl.ds(width, width)] = jnp.where(core == 0, other, mine)


def spread_hidden(meta, table, near, far):
    sources, capacity, width = near.shape
    tokens = table.shape[-1]
    return pl.pallas_call(
        functools.partial(spread_kernel, capacity),
        grid_spec=pltpu.PrefetchScalarGridSpec(
            num_scalar_prefetch=1,
            grid=(sources,),
            in_specs=[
                pl.BlockSpec((1, TABLE_ROWS, tokens), lambda p, meta: (p, 0, 0)),
                pl.BlockSpec((1, capacity, width), lambda p, meta: (meta[2 + p], 0, 0)),
                pl.BlockSpec((1, capacity, width), lambda p, meta: (meta[2 + p], 0, 0)),
            ],
            out_specs=pl.BlockSpec((1, tokens, 2 * width), lambda p, meta: (meta[2 + p], 0, 0)),
        ),
        out_shape=jax.ShapeDtypeStruct((sources, tokens, 2 * width), BF),
        cost_estimate=pl.CostEstimate(
            flops=8 * sources * tokens * capacity * width, bytes_accessed=14 * MIB, transcendentals=0
        ),
        name="spread_hidden",
    )(meta, table, near, far)


def product_kernel(piece_count, order, *refs):
    pieces = refs[:piece_count]
    spread, out, held = refs[piece_count:]
    tokens = spread.shape[1]
    total = spread.shape[0]

    @pl.when(pl.program_id(0) == 0)
    def _():
        for p in range(total):
            held[pl.ds(p * tokens, tokens), :] = spread[order[p]]

    left = jnp.concatenate([piece[k] for piece in pieces for k in range(piece.shape[0])], axis=1)
    out[0] = jnp.dot(left, held[...], preferred_element_type=F32)


def products(order, pieces, spread, first, steps, rows):
    sources, tokens, columns = spread.shape
    return pl.pallas_call(
        functools.partial(product_kernel, len(pieces)),
        grid_spec=pltpu.PrefetchScalarGridSpec(
            num_scalar_prefetch=1,
            grid=(steps,),
            in_specs=[
                pl.BlockSpec((piece.shape[0], rows, tokens), lambda i, order: (0, first + i, 0)) for piece in pieces
            ]
            + [pl.BlockSpec((sources, tokens, columns), lambda i, order: (0, 0, 0))],
            out_specs=pl.BlockSpec((1, rows, columns), lambda i, order: (i, 0, 0)),
            scratch_shapes=[pltpu.VMEM((sources * tokens, columns), BF)],
        ),
        out_shape=jax.ShapeDtypeStruct((steps, rows, columns), F32),
        cost_estimate=pl.CostEstimate(
            flops=2 * steps * rows * sources * tokens * columns, bytes_accessed=10 * MIB, transcendentals=0
        ),
        compiler_params=pltpu.CompilerParams(vmem_limit_bytes=40 * MIB),
        name="products",
    )(order, *pieces, spread)


STRIP = 8


def strip_update(first, second_layer, grad, weight, moment, second):
    units_total = second_layer.shape[1]
    ones = jnp.ones(grad.shape, F32)
    grad = grad * (1.0 / LOSS_SCALE)
    moment_new = FIRST_DECAY * moment + (1.0 - FIRST_DECAY) * grad
    second_new = SECOND_DECAY * second + (1.0 - SECOND_DECAY) * grad * grad
    inverse = lax.rsqrt(second_new + EPSILON)
    features = [grad, moment_new, grad * inverse, moment_new * inverse, WEIGHT_FEATURE * weight]
    high = [f.astype(BF).astype(F32) for f in features]
    low = [f - h for f, h in zip(features, high)]
    stack = jnp.concatenate(high + low + high + [ones, ones, ones], axis=0).astype(BF)
    units = jnp.dot(first[...], stack, preferred_element_type=F32)
    net0 = jnp.zeros(grad.shape, F32)
    net1 = jnp.zeros(grad.shape, F32)
    for j in range(units_total):
        unit = jnp.maximum(units[j * STRIP : (j + 1) * STRIP, :], 0.0)
        net0 = net0 + second_layer[0, j] * unit
        net1 = net1 + second_layer[1, j] * unit
    return net0 * jnp.exp(jnp.tanh(net1)), moment_new, second_new


def update_kernel(core, first, second_layer, mine, other, weight, moment, second, *rest):
    outs = rest[-3:]
    is_mine = pl.program_id(0) == core[0]

    def body(i, carry):
        at = pl.ds(pl.multiple_of(i * 2 * STRIP, 2 * STRIP), 2 * STRIP)
        grad = jnp.where(is_mine, mine[at, :], other[at, :])
        values = [grad] + [ref[at, :].astype(F32) for ref in (weight, moment, second)]
        parts = [
            strip_update(first, second_layer, *(v[h * STRIP : (h + 1) * STRIP, :] for v in values)) for h in range(2)
        ]
        for k, ref in enumerate(outs):
            ref[at, :] = jnp.concatenate([part[k] for part in parts], axis=0).astype(BF)
        return carry

    steps = mine.shape[0] // (2 * STRIP)
    lax.fori_loop(0, steps, body, 0, unroll=7 if steps % 7 == 0 else 1)


def update(core, first, mlp_out, mine, other, weight, moment, second, part, earlier):
    rows, columns = mine.shape
    wide = 256
    grads = pl.BlockSpec((rows, wide), lambda c, j, core: (0, j))
    spec = pl.BlockSpec((rows, wide), lambda c, j, core: (2 * c + part, j))
    shape = jax.ShapeDtypeStruct(weight.shape, BF)
    return pl.pallas_call(
        update_kernel,
        grid_spec=pltpu.PrefetchScalarGridSpec(
            num_scalar_prefetch=1,
            grid=(2, columns // wide),
            in_specs=[
                pl.BlockSpec(first.shape, lambda c, j, core: (0, 0)),
                pl.BlockSpec(memory_space=pltpu.SMEM),
                grads,
                grads,
                spec,
                spec,
                spec,
            ]
            + [pl.BlockSpec(memory_space=pl.ANY)] * len(earlier),
            out_specs=[spec, spec, spec],
        ),
        out_shape=[shape, shape, shape],
        input_output_aliases={8 + k: k for k in range(len(earlier))},
        cost_estimate=pl.CostEstimate(flops=10**10, bytes_accessed=6 * MIB, transcendentals=10**6),
        name="update",
    )(core, first, mlp_out, mine, other, weight, moment, second, *earlier)


def first_layer(mlp_in, mlp_bias):
    def split(v):
        high = v.astype(BF).astype(F32)
        middle = (v - high).astype(BF).astype(F32)
        return high, middle, v - high - middle

    high, low, _ = split(mlp_in)
    bias = jnp.stack(split(mlp_bias), axis=1)
    table = jnp.concatenate([high, high, low, bias], axis=1)
    wide = table[:, None, :, None] * jnp.eye(STRIP, dtype=F32)[None, :, None, :]
    return wide.reshape(table.shape[0] * STRIP, table.shape[1] * STRIP).astype(BF)


def per_device(
    grad_out, route_weight, expert_ids, hidden, weight, moment, second, mlp_in, mlp_bias, mlp_out
):
    expert = lax.axis_index("expert")
    place = lax.axis_index("dp")
    core = lax.axis_index("tensor")
    groups = lax.axis_size("dp")
    cores = lax.axis_size("tensor")
    tokens = grad_out.shape[0]
    sources = hidden.shape[2]
    rows = weight.shape[1] // cores
    half = rows // 2

    near = hidden[0, 0]
    far = lax.ppermute(near, "tensor", [(0, 1), (1, 0)])

    features = grad_out.T.reshape(groups // cores, cores, rows, tokens)
    keep = lax.dynamic_index_in_dim(features, core, 1, keepdims=False)
    give = lax.dynamic_index_in_dim(features, 1 - core, 1, keepdims=False)
    slices = jnp.concatenate([keep, lax.ppermute(give, "tensor", [(0, 1), (1, 0)])], axis=0)
    shift = place + core * (groups // cores)
    ordered = [
        lax.dynamic_index_in_dim(slices, (shift + offset) % groups, 0, keepdims=False) for offset in OFFSETS
    ]

    ids = expert_ids.T.astype(BF)
    weights = route_weight.T
    weight_high = weights.astype(BF)
    weight_low = (weights - weight_high.astype(F32)).astype(BF)
    table = jnp.concatenate([ids, weight_high, weight_low, jnp.zeros_like(ids)], axis=0)
    tables = gather_tables(table[None])
    sequence = expert ^ jnp.arange(sources, dtype=jnp.int32)
    meta = jnp.concatenate([jnp.stack([expert, core]).astype(jnp.int32), sequence])
    spread = spread_hidden(meta, tables, near, far)

    block_a = jnp.concatenate([ordered[0], ordered[1][:half]], axis=0)
    block_b = jnp.concatenate([ordered[1][half:], ordered[2]], axis=0)
    late = lax.all_gather(jnp.concatenate(ordered[3:], axis=0), "expert", axis=0)
    pieces_a, pieces_b = torus_pair_gather(block_a, block_b)

    part_a = products(piece_sources(expert, True), pieces_a, spread, 0, 1, 3 * half)[0]
    part_b = products(piece_sources(expert, False), pieces_b, spread, 0, 1, 3 * half)[0]
    plain = jnp.arange(sources, dtype=jnp.int32)
    part_c = products(plain, (late,), spread, 0, 2, rows)
    part_d = products(plain, (late,), spread, 2, 3, rows)
    parts = {
        4: (part_a[:half], part_a[half:rows]),
        3: (part_a[rows:], part_b[:half]),
        -3: (part_b[half:rows], part_b[rows:]),
    }
    for offset, block in zip(OFFSETS[3:], (part_c[0], part_c[1], part_d[0], part_d[1], part_d[2])):
        parts[offset] = (block[:half], block[half:])

    rise = [(i, (i + 1) % groups) for i in range(groups)]
    fall = [(i, (i - 1) % groups) for i in range(groups)]
    chains = {
        (0, 1): [4, 3, 2, 1],
        (1, -1): [4, -3, -2, -1],
        (0, -1): [-3, -2, -1],
        (1, 1): [3, 2, 1],
    }
    moving = {}
    for step in range(4):
        for (part, way), chain in chains.items():
            at = step - (4 - len(chain))
            if at < 0:
                continue
            value = parts[chain[at]][part]
            if at > 0:
                value = moving[part, way].astype(F32) + value
            moving[part, way] = lax.ppermute(value.astype(BF), "dp", rise if way == 1 else fall)

    first = first_layer(mlp_in, mlp_bias)
    columns = hidden.shape[-1]
    outs = ()
    for part in range(2):
        grad = moving[part, 1].astype(F32) + moving[part, -1].astype(F32) + parts[0][part]
        mine = lax.dynamic_slice_in_dim(grad, core * columns, columns, axis=1)
        given = lax.dynamic_slice_in_dim(grad, (1 - core) * columns, columns, axis=1)
        other = lax.ppermute(given, "tensor", [(0, 1), (1, 0)])
        outs = update(
            core.astype(jnp.int32)[None], first, mlp_out, mine, other, weight[0], moment[0], second[0], part, outs
        )
    return tuple(out[None] for out in outs)


def solution(mesh):
    split = P("expert", "dp", "tensor")
    return jax.shard_map(
        per_device,
        mesh=mesh,
        in_specs=(
            P(("expert", "dp"), "tensor"),
            P(("expert", "dp"), None),
            P(("expert", "dp"), None),
            P("expert", "dp", None, None, "tensor"),
            split,
            split,
            split,
            P(),
            P(),
            P(),
        ),
        out_specs=(split, split, split),
        check_vma=False,
    )
```

```python
import functools

import jax
import jax.numpy as jnp
from jax import lax
from jax.experimental import pallas as pl
from jax.experimental.pallas import tpu as pltpu
from jax.sharding import PartitionSpec as P

BF = jnp.bfloat16
F32 = jnp.float32

LOSS_SCALE = 16.0
FIRST_DECAY = 0.9
SECOND_DECAY = 0.95
WEIGHT_FEATURE = 32.0
EPSILON = 1e-08

OFFSETS = (4, 3, -3, 2, -2, 1, -1, 0)
SIDE = 4
TABLE_ROWS = 32
MIB = 1 << 20


def along_x(k):
    return [(y * SIDE + x, y * SIDE + (x + k) % SIDE) for y in range(SIDE) for x in range(SIDE)]


def along_y(k):
    return [(y * SIDE + x, (y + k) % SIDE * SIDE + x) for y in range(SIDE) for x in range(SIDE)]


def after(values, others):
    tied = lax.optimization_barrier(tuple(values) + tuple(others))
    return tied[: len(values)], tied[len(values) :]


def ring_pair_gather(block_a, pairs_a, block_b, pairs_b, beside):
    blocks = ((block_a, pairs_a), (block_b, pairs_b))
    near = []
    for block, pairs in blocks:
        near.append(lax.ppermute(block, "expert", pairs(1)))
        near.append(lax.ppermute(block, "expert", pairs(-1)))
    near, beside = after(near, beside)
    far = []
    for k, (block, pairs) in enumerate(blocks):
        half = block.shape[0] // 2
        far.append(lax.ppermute(near[2 * k][:half], "expert", pairs(1)))
        far.append(lax.ppermute(near[2 * k + 1][half:], "expert", pairs(-1)))
    return [(block, near[2 * k], near[2 * k + 1], far[2 * k], far[2 * k + 1]) for k, (block, _) in enumerate(blocks)], beside


def torus_pair_gather(block_a, block_b, beside):
    lines, beside = ring_pair_gather(block_a, along_x, block_b, along_y, beside)
    stacks = [
        jnp.stack([own, behind, ahead, jnp.concatenate([first, second], axis=0)])
        for own, behind, ahead, first, second in lines
    ]
    stacks, _ = after(stacks, ())
    mine = stacks[0][:, -TABLE_ROWS:]
    opposite = lax.ppermute(mine, "expert", along_y(2))
    (pieces_a, pieces_b), (opposite,) = ring_pair_gather(stacks[0], along_y, stacks[1], along_x, (opposite,))
    tables = jnp.concatenate([mine, pieces_a[1][:, -TABLE_ROWS:], pieces_a[2][:, -TABLE_ROWS:], opposite], axis=0)
    return pieces_a, pieces_b, tables, beside


def piece_sources(expert, inner_is_x):
    y, x = expert // SIDE, expert % SIDE
    offsets = (0, -1, 1, 2)
    out = []
    for outer in offsets:
        for inner in offsets:
            dx, dy = (inner, outer) if inner_is_x else (outer, inner)
            out.append((y + dy) % SIDE * SIDE + (x + dx) % SIDE)
    return jnp.stack(out).astype(jnp.int32)


GROUP = 4


def spread_kernel(capacity, meta, table, near, far, out):
    expert, core = meta[0], meta[1]
    tokens = table.shape[-1]
    width = near.shape[-1]
    earlier = (
        lax.broadcasted_iota(jnp.int32, (tokens, tokens), 0)
        < lax.broadcasted_iota(jnp.int32, (tokens, tokens), 1)
    ).astype(F32).astype(BF)
    place = lax.broadcasted_iota(jnp.int32, (capacity, tokens), 0).astype(F32)
    dims = (((0,), (0,)), ((), ()))
    for k in range(GROUP):
        entry = table[meta[2 + pl.program_id(0) * GROUP + k]].astype(F32)
        ids = entry[0:8, :]
        weight = entry[8:16, :] + entry[16:24, :]
        hit = (ids == expert.astype(F32)).astype(F32)
        named = jnp.sum(hit, axis=0, keepdims=True)
        scale = jnp.sum(hit * weight, axis=0, keepdims=True)
        slot = jnp.dot(
            jnp.broadcast_to(named, (16, tokens)).astype(BF), earlier, preferred_element_type=F32
        )[0:1, :]
        slot = jnp.where(named > 0.5, slot, -1.0)
        chosen = jnp.where(place == slot, jnp.broadcast_to(scale, (capacity, tokens)), 0.0)
        high = chosen.astype(BF)
        low = (chosen - high.astype(F32)).astype(BF)
        left = jnp.concatenate([high, low], axis=0)
        mine = lax.dot_general(
            left, jnp.concatenate([near[k], near[k]], axis=0), dims, preferred_element_type=F32
        ).astype(BF)
        other = lax.dot_general(
            left, jnp.concatenate([far[k], far[k]], axis=0), dims, preferred_element_type=F32
        ).astype(BF)
        out[k, :, pl.ds(0, width)] = jnp.where(core == 0, mine, other)
        out[k, :, pl.ds(width, width)] = jnp.where(core == 0, other, mine)


def spread_hidden(meta, table, near, far):
    sources, capacity, width = near.shape
    tokens = table.shape[-1]
    part = pl.BlockSpec((GROUP, capacity, width), lambda p, meta: (p, 0, 0))
    return pl.pallas_call(
        functools.partial(spread_kernel, capacity),
        grid_spec=pltpu.PrefetchScalarGridSpec(
            num_scalar_prefetch=1,
            grid=(sources // GROUP,),
            in_specs=[pl.BlockSpec(table.shape, lambda p, meta: (0, 0, 0)), part, part],
            out_specs=pl.BlockSpec((GROUP, tokens, 2 * width), lambda p, meta: (p, 0, 0)),
        ),
        out_shape=jax.ShapeDtypeStruct((sources, tokens, 2 * width), BF),
        cost_estimate=pl.CostEstimate(
            flops=8 * sources * tokens * capacity * width, bytes_accessed=14 * MIB, transcendentals=0
        ),
        compiler_params=pltpu.CompilerParams(vmem_limit_bytes=32 * MIB),
        name="spread_hidden",
    )(meta, table, near, far)


def product_kernel(piece_count, order, *refs):
    count = (len(refs) - 2) // (piece_count + 1)
    spread, outs, held = refs[piece_count * count], refs[piece_count * count + 1 : -1], refs[-1]
    total, tokens, _ = spread.shape
    for p in range(total):
        held[pl.ds(p * tokens, tokens), :] = spread[order[p]]
    lefts = []
    for i in range(count):
        pieces = refs[i * piece_count : (i + 1) * piece_count]
        lefts.append(jnp.concatenate([piece[k] for piece in pieces for k in range(piece.shape[0])], axis=1))
    result = jnp.dot(jnp.concatenate(lefts, axis=0), held[...], preferred_element_type=F32).astype(BF)
    rows = outs[0].shape[0]
    for i, out in enumerate(outs):
        out[...] = result[i * rows : (i + 1) * rows, :]


def products(order, pieces, spread, blocks, half):
    sources, tokens, columns = spread.shape
    return pl.pallas_call(
        functools.partial(product_kernel, len(pieces)),
        grid_spec=pltpu.PrefetchScalarGridSpec(
            num_scalar_prefetch=1,
            grid=(1,),
            in_specs=[
                pl.BlockSpec((piece.shape[0], half, tokens), lambda i, order, block=block: (0, block, 0))
                for block in blocks
                for piece in pieces
            ]
            + [pl.BlockSpec((sources, tokens, columns), lambda i, order: (0, 0, 0))],
            out_specs=[pl.BlockSpec((half, columns), lambda i, order: (0, 0))] * len(blocks),
            scratch_shapes=[pltpu.VMEM((sources * tokens, columns), BF)],
        ),
        out_shape=[jax.ShapeDtypeStruct((half, columns), BF)] * len(blocks),
        cost_estimate=pl.CostEstimate(
            flops=2 * len(blocks) * half * sources * tokens * columns, bytes_accessed=10 * MIB, transcendentals=0
        ),
        compiler_params=pltpu.CompilerParams(vmem_limit_bytes=48 * MIB),
        name="products",
    )(order, *pieces * len(blocks), spread)


STRIP = 8


def strip_update(first, second_layer, grad, weight, moment, second):
    units_total = second_layer.shape[1]
    ones = jnp.ones(grad.shape, F32)
    grad = grad * (1.0 / LOSS_SCALE)
    moment_new = FIRST_DECAY * moment + (1.0 - FIRST_DECAY) * grad
    second_new = SECOND_DECAY * second + (1.0 - SECOND_DECAY) * grad * grad
    inverse = lax.rsqrt(second_new + EPSILON)
    features = [grad, moment_new, grad * inverse, moment_new * inverse, WEIGHT_FEATURE * weight]
    high = [f.astype(BF).astype(F32) for f in features]
    low = [f - h for f, h in zip(features, high)]
    stack = jnp.concatenate(high + low + high + [ones, ones, ones], axis=0).astype(BF)
    units = jnp.dot(first[...], stack, preferred_element_type=F32)
    net0 = jnp.zeros(grad.shape, F32)
    net1 = jnp.zeros(grad.shape, F32)
    for j in range(units_total):
        unit = jnp.maximum(units[j * STRIP : (j + 1) * STRIP, :], 0.0)
        net0 = net0 + second_layer[0, j] * unit
        net1 = net1 + second_layer[1, j] * unit
    return net0 * jnp.exp(jnp.tanh(net1)), moment_new, second_new


def update_kernel(core, first, second_layer, rising, falling, own, other, weight, moment, second, *rest):
    outs = rest[-3:]
    is_mine = pl.program_id(0) == core[0]

    def body(i, carry):
        at = pl.ds(pl.multiple_of(i * 2 * STRIP, 2 * STRIP), 2 * STRIP)
        mine = rising[at, :].astype(F32) + falling[at, :].astype(F32) + own[at, :].astype(F32)
        grad = jnp.where(is_mine, mine, other[at, :])
        values = [grad] + [ref[at, :].astype(F32) for ref in (weight, moment, second)]
        parts = [
            strip_update(first, second_layer, *(v[h * STRIP : (h + 1) * STRIP, :] for v in values)) for h in range(2)
        ]
        for k, ref in enumerate(outs):
            ref[at, :] = jnp.concatenate([part[k] for part in parts], axis=0).astype(BF)
        return carry

    steps = other.shape[0] // (2 * STRIP)
    lax.fori_loop(0, steps, body, 0, unroll=7 if steps % 7 == 0 else 1)


def update(core, first, mlp_out, sums, other, weight, moment, second, part, earlier):
    rows, columns = other.shape
    wide = 256
    across = columns // wide
    mine = pl.BlockSpec((rows, wide), lambda c, j, core: (0, core[0] * across + j))
    given = pl.BlockSpec((rows, wide), lambda c, j, core: (0, j))
    spec = pl.BlockSpec((rows, wide), lambda c, j, core: (2 * c + part, j))
    shape = jax.ShapeDtypeStruct(weight.shape, BF)
    return pl.pallas_call(
        update_kernel,
        grid_spec=pltpu.PrefetchScalarGridSpec(
            num_scalar_prefetch=1,
            grid=(2, across),
            in_specs=[
                pl.BlockSpec(first.shape, lambda c, j, core: (0, 0)),
                pl.BlockSpec(memory_space=pltpu.SMEM),
                mine,
                mine,
                mine,
                given,
                spec,
                spec,
                spec,
            ]
            + [pl.BlockSpec(memory_space=pl.ANY)] * len(earlier),
            out_specs=[spec, spec, spec],
        ),
        out_shape=[shape, shape, shape],
        input_output_aliases={10 + k: k for k in range(len(earlier))},
        cost_estimate=pl.CostEstimate(flops=10**10, bytes_accessed=6 * MIB, transcendentals=10**6),
        name="update",
    )(core, first, mlp_out, *sums, other, weight, moment, second, *earlier)


def first_layer(mlp_in, mlp_bias):
    def split(v):
        high = v.astype(BF).astype(F32)
        middle = (v - high).astype(BF).astype(F32)
        return high, middle, v - high - middle

    high, low, _ = split(mlp_in)
    bias = jnp.stack(split(mlp_bias), axis=1)
    table = jnp.concatenate([high, high, low, bias], axis=1)
    wide = table[:, None, :, None] * jnp.eye(STRIP, dtype=F32)[None, :, None, :]
    return wide.reshape(table.shape[0] * STRIP, table.shape[1] * STRIP).astype(BF)


def per_device(
    grad_out, route_weight, expert_ids, hidden, weight, moment, second, mlp_in, mlp_bias, mlp_out
):
    expert = lax.axis_index("expert")
    place = lax.axis_index("dp")
    core = lax.axis_index("tensor")
    groups = lax.axis_size("dp")
    cores = lax.axis_size("tensor")
    tokens = grad_out.shape[0]
    sources = hidden.shape[2]
    rows = weight.shape[1] // cores
    half = rows // 2

    near = hidden[0, 0]
    far = lax.ppermute(near, "tensor", [(0, 1), (1, 0)])

    features = grad_out.T.reshape(groups // cores, cores, rows, tokens)
    keep = lax.dynamic_index_in_dim(features, core, 1, keepdims=False)
    give = lax.dynamic_index_in_dim(features, 1 - core, 1, keepdims=False)
    slices = jnp.concatenate([keep, lax.ppermute(give, "tensor", [(0, 1), (1, 0)])], axis=0)
    shift = place + core * (groups // cores)
    ordered = [
        lax.dynamic_index_in_dim(slices, (shift + offset) % groups, 0, keepdims=False) for offset in OFFSETS
    ]

    ids = expert_ids.T.astype(BF)
    weights = route_weight.T
    weight_high = weights.astype(BF)
    weight_low = (weights - weight_high.astype(F32)).astype(BF)
    table = jnp.concatenate([ids, weight_high, weight_low, jnp.zeros_like(ids)], axis=0)
    first = first_layer(mlp_in, mlp_bias)

    block_a = jnp.concatenate([ordered[0], ordered[1][:half], table], axis=0)
    block_b = jnp.concatenate([ordered[1][half:], ordered[2]], axis=0)
    soon = jnp.concatenate([ordered[3], ordered[4]] + [block[:half] for block in ordered[5:]], axis=0)
    late = jnp.concatenate([block[half:] for block in ordered[5:]], axis=0)
    soon, late = (lax.all_gather(block, "expert", axis=0) for block in (soon, late))
    pieces_a, pieces_b, tables, (first,) = torus_pair_gather(block_a, block_b, (first,))
    order_a, order_b = piece_sources(expert, True), piece_sources(expert, False)
    plain = jnp.arange(sources, dtype=jnp.int32)
    places = jnp.sum(jnp.where(order_a[None, :] == plain[:, None], plain[None, :], 0), axis=1)
    meta = jnp.concatenate([jnp.stack([expert, core]).astype(jnp.int32), places.astype(jnp.int32)])
    spread = spread_hidden(meta, tables, near, far)

    parts = {}

    def make(order, pieces, names):
        made = products(order, pieces, spread, [name[0] for name in names], half)
        parts.update({name[1:]: value for name, value in zip(names, made)})

    make(order_a, pieces_a, [(0, 4, 0), (1, 4, 1), (2, 3, 0)])
    make(order_b, pieces_b, [(0, 3, 1), (1, -3, 0), (2, -3, 1)])
    make(plain, (soon,), [(0, 2, 0), (1, 2, 1), (2, -2, 0), (3, -2, 1)])
    make(plain, (soon,), [(4, 1, 0), (5, -1, 0), (6, 0, 0)])
    make(plain, (late,), [(0, 1, 1), (1, -1, 1), (2, 0, 1)])

    rise = [(i, (i + 1) % groups) for i in range(groups)]
    fall = [(i, (i - 1) % groups) for i in range(groups)]
    chains = {
        (0, 1): [4, 3, 2, 1],
        (1, -1): [4, -3, -2, -1],
        (0, -1): [-3, -2, -1],
        (1, 1): [3, 2, 1],
    }
    moving = {}
    for step in range(4):
        for (part, way), chain in chains.items():
            at = step - (4 - len(chain))
            if at < 0:
                continue
            value = parts[chain[at], part]
            if at > 0:
                value = (moving[part, way].astype(F32) + value.astype(F32)).astype(BF)
            moving[part, way] = lax.ppermute(value, "dp", rise if way == 1 else fall)

    columns = hidden.shape[-1]
    outs = ()
    for part in range(2):
        moved = (moving[part, 1], moving[part, -1])
        if outs:
            moved, outs = after(moved, outs)
        sums = moved + (parts[0, part],)
        given = sum(
            lax.dynamic_slice_in_dim(v, (1 - core) * columns, columns, axis=1).astype(F32) for v in sums
        )
        other = lax.ppermute(given, "tensor", [(0, 1), (1, 0)])
        outs = update(
            core.astype(jnp.int32)[None], first, mlp_out, sums, other, weight[0], moment[0], second[0], part, outs
        )
    return tuple(out[None] for out in outs)


def solution(mesh):
    split = P("expert", "dp", "tensor")
    return jax.shard_map(
        per_device,
        mesh=mesh,
        in_specs=(
            P(("expert", "dp"), "tensor"),
            P(("expert", "dp"), None),
            P(("expert", "dp"), None),
            P("expert", "dp", None, None, "tensor"),
            split,
            split,
            split,
            P(),
            P(),
            P(),
        ),
        out_specs=(split, split, split),
        check_vma=False,
    )
```

```python
import functools

import jax
import jax.numpy as jnp
from jax import lax
from jax.experimental import pallas as pl
from jax.experimental.pallas import tpu as pltpu
from jax.sharding import PartitionSpec as P

BF = jnp.bfloat16
F32 = jnp.float32

LOSS_SCALE = 16.0
FIRST_DECAY = 0.9
SECOND_DECAY = 0.95
WEIGHT_FEATURE = 32.0
EPSILON = 1e-08

OFFSETS = (4, 3, -3, 2, -2, 1, -1, 0)
SIDE = 4
TABLE_ROWS = 32
MIB = 1 << 20


def along_x(k):
    return [(y * SIDE + x, y * SIDE + (x + k) % SIDE) for y in range(SIDE) for x in range(SIDE)]


def along_y(k):
    return [(y * SIDE + x, (y + k) % SIDE * SIDE + x) for y in range(SIDE) for x in range(SIDE)]


def after(values, others):
    tied = lax.optimization_barrier(tuple(values) + tuple(others))
    return tied[: len(values)], tied[len(values) :]


def ring_pair_gather(block_a, pairs_a, block_b, pairs_b, beside):
    blocks = ((block_a, pairs_a), (block_b, pairs_b))
    near = []
    for block, pairs in blocks:
        near.append(lax.ppermute(block, "expert", pairs(1)))
        near.append(lax.ppermute(block, "expert", pairs(-1)))
    near, beside = after(near, beside)
    far = []
    for k, (block, pairs) in enumerate(blocks):
        half = block.shape[0] // 2
        far.append(lax.ppermute(near[2 * k][:half], "expert", pairs(1)))
        far.append(lax.ppermute(near[2 * k + 1][half:], "expert", pairs(-1)))
    return [(block, near[2 * k], near[2 * k + 1], far[2 * k], far[2 * k + 1]) for k, (block, _) in enumerate(blocks)], beside


def torus_pair_gather(block_a, block_b, beside):
    lines, beside = ring_pair_gather(block_a, along_x, block_b, along_y, beside)
    stacks = [
        jnp.stack([own, behind, ahead, jnp.concatenate([first, second], axis=0)])
        for own, behind, ahead, first, second in lines
    ]
    stacks, _ = after(stacks, ())
    mine = stacks[0][:, -TABLE_ROWS:]
    opposite = lax.ppermute(mine, "expert", along_y(2))
    (pieces_a, pieces_b), (opposite,) = ring_pair_gather(stacks[0], along_y, stacks[1], along_x, (opposite,))
    tables = jnp.concatenate([mine, pieces_a[1][:, -TABLE_ROWS:], pieces_a[2][:, -TABLE_ROWS:], opposite], axis=0)
    return pieces_a, pieces_b, tables, beside


def piece_sources(expert, inner_is_x):
    y, x = expert // SIDE, expert % SIDE
    offsets = (0, -1, 1, 2)
    out = []
    for outer in offsets:
        for inner in offsets:
            dx, dy = (inner, outer) if inner_is_x else (outer, inner)
            out.append((y + dy) % SIDE * SIDE + (x + dx) % SIDE)
    return jnp.stack(out).astype(jnp.int32)


GROUP = 4


def spread_kernel(capacity, meta, table, near, far, out):
    expert, core = meta[0], meta[1]
    tokens = table.shape[-1]
    width = near.shape[-1]
    earlier = (
        lax.broadcasted_iota(jnp.int32, (tokens, tokens), 0)
        < lax.broadcasted_iota(jnp.int32, (tokens, tokens), 1)
    ).astype(F32).astype(BF)
    place = lax.broadcasted_iota(jnp.int32, (capacity, tokens), 0).astype(F32)
    dims = (((0,), (0,)), ((), ()))
    for k in range(GROUP):
        entry = table[meta[2 + pl.program_id(0) * GROUP + k]].astype(F32)
        ids = entry[0:8, :]
        weight = entry[8:16, :] + entry[16:24, :]
        hit = (ids == expert.astype(F32)).astype(F32)
        named = jnp.sum(hit, axis=0, keepdims=True)
        scale = jnp.sum(hit * weight, axis=0, keepdims=True)
        slot = jnp.dot(
            jnp.broadcast_to(named, (16, tokens)).astype(BF), earlier, preferred_element_type=F32
        )[0:1, :]
        slot = jnp.where(named > 0.5, slot, -1.0)
        chosen = jnp.where(place == slot, jnp.broadcast_to(scale, (capacity, tokens)), 0.0)
        high = chosen.astype(BF)
        low = (chosen - high.astype(F32)).astype(BF)
        left = jnp.concatenate([high, low], axis=0)
        mine = lax.dot_general(
            left, jnp.concatenate([near[k], near[k]], axis=0), dims, preferred_element_type=F32
        ).astype(BF)
        other = lax.dot_general(
            left, jnp.concatenate([far[k], far[k]], axis=0), dims, preferred_element_type=F32
        ).astype(BF)
        out[k, :, pl.ds(pl.multiple_of(core * width, width), width)] = mine
        out[k, :, pl.ds(pl.multiple_of((1 - core) * width, width), width)] = other


def spread_hidden(meta, table, near, far):
    sources, capacity, width = near.shape
    tokens = table.shape[-1]
    part = pl.BlockSpec((GROUP, capacity, width), lambda p, meta: (p, 0, 0))
    return pl.pallas_call(
        functools.partial(spread_kernel, capacity),
        grid_spec=pltpu.PrefetchScalarGridSpec(
            num_scalar_prefetch=1,
            grid=(sources // GROUP,),
            in_specs=[pl.BlockSpec(table.shape, lambda p, meta: (0, 0, 0)), part, part],
            out_specs=pl.BlockSpec((GROUP, tokens, 2 * width), lambda p, meta: (p, 0, 0)),
        ),
        out_shape=jax.ShapeDtypeStruct((sources, tokens, 2 * width), BF),
        cost_estimate=pl.CostEstimate(
            flops=8 * sources * tokens * capacity * width, bytes_accessed=14 * MIB, transcendentals=0
        ),
        compiler_params=pltpu.CompilerParams(vmem_limit_bytes=32 * MIB),
        name="spread_hidden",
    )(meta, table, near, far)


def product_kernel(piece_count, order, *refs):
    count = (len(refs) - 2) // (piece_count + 1)
    spread, outs, held = refs[piece_count * count], refs[piece_count * count + 1 : -1], refs[-1]
    total, tokens, _ = spread.shape
    for p in range(total):
        held[pl.ds(p * tokens, tokens), :] = spread[order[p]]
    lefts = []
    for i in range(count):
        pieces = refs[i * piece_count : (i + 1) * piece_count]
        lefts.append(jnp.concatenate([piece[k] for piece in pieces for k in range(piece.shape[0])], axis=1))
    result = jnp.dot(jnp.concatenate(lefts, axis=0), held[...], preferred_element_type=F32).astype(BF)
    rows = outs[0].shape[0]
    for i, out in enumerate(outs):
        out[...] = result[i * rows : (i + 1) * rows, :]


def products(order, pieces, spread, blocks, half):
    sources, tokens, columns = spread.shape
    return pl.pallas_call(
        functools.partial(product_kernel, len(pieces)),
        grid_spec=pltpu.PrefetchScalarGridSpec(
            num_scalar_prefetch=1,
            grid=(1,),
            in_specs=[
                pl.BlockSpec((piece.shape[0], half, tokens), lambda i, order, block=block: (0, block, 0))
                for block in blocks
                for piece in pieces
            ]
            + [pl.BlockSpec((sources, tokens, columns), lambda i, order: (0, 0, 0))],
            out_specs=[pl.BlockSpec((half, columns), lambda i, order: (0, 0))] * len(blocks),
            scratch_shapes=[pltpu.VMEM((sources * tokens, columns), BF)],
        ),
        out_shape=[jax.ShapeDtypeStruct((half, columns), BF)] * len(blocks),
        cost_estimate=pl.CostEstimate(
            flops=2 * len(blocks) * half * sources * tokens * columns, bytes_accessed=10 * MIB, transcendentals=0
        ),
        compiler_params=pltpu.CompilerParams(vmem_limit_bytes=48 * MIB),
        name="products",
    )(order, *pieces * len(blocks), spread)


STRIP = 8


def strip_update(first, second_layer, grad, weight, moment, second):
    units_total = second_layer.shape[1]
    ones = jnp.ones(grad.shape, F32)
    grad = grad * (1.0 / LOSS_SCALE)
    moment_new = FIRST_DECAY * moment + (1.0 - FIRST_DECAY) * grad
    second_new = SECOND_DECAY * second + (1.0 - SECOND_DECAY) * grad * grad
    inverse = lax.rsqrt(second_new + EPSILON)
    features = [grad, moment_new, grad * inverse, moment_new * inverse, WEIGHT_FEATURE * weight]
    high = [f.astype(BF).astype(F32) for f in features]
    low = [f - h for f, h in zip(features, high)]
    stack = jnp.concatenate(high + low + high + [ones, ones, ones], axis=0).astype(BF)
    units = jnp.dot(first[...], stack, preferred_element_type=F32)
    net0 = jnp.zeros(grad.shape, F32)
    net1 = jnp.zeros(grad.shape, F32)
    for j in range(units_total):
        unit = jnp.maximum(units[j * STRIP : (j + 1) * STRIP, :], 0.0)
        net0 = net0 + second_layer[0, j] * unit
        net1 = net1 + second_layer[1, j] * unit
    return net0 * jnp.exp(jnp.tanh(net1)), moment_new, second_new


def update_kernel(core, table, second_layer, rising, falling, own, other, weight, moment, second, *rest):
    outs, first = rest[-4:-1], rest[-1]
    is_mine = pl.program_id(0) == core[0]

    @pl.when((pl.program_id(0) == 0) & (pl.program_id(1) == 0))
    def _():
        first[...] = widen(table[...])


    def body(i, carry):
        at = pl.ds(pl.multiple_of(i * 2 * STRIP, 2 * STRIP), 2 * STRIP)
        mine = rising[at, :].astype(F32) + falling[at, :].astype(F32) + own[at, :].astype(F32)
        grad = jnp.where(is_mine, mine, other[at, :])
        values = [grad] + [ref[at, :].astype(F32) for ref in (weight, moment, second)]
        parts = [
            strip_update(first, second_layer, *(v[h * STRIP : (h + 1) * STRIP, :] for v in values)) for h in range(2)
        ]
        for k, ref in enumerate(outs):
            ref[at, :] = jnp.concatenate([part[k] for part in parts], axis=0).astype(BF)
        return carry

    steps = other.shape[0] // (2 * STRIP)
    lax.fori_loop(0, steps, body, 0, unroll=7 if steps % 7 == 0 else 1)


def update(core, first, mlp_out, sums, other, weight, moment, second, part, earlier):
    rows, columns = other.shape
    wide = 256
    across = columns // wide
    mine = pl.BlockSpec((rows, wide), lambda c, j, core: (0, core[0] * across + j))
    given = pl.BlockSpec((rows, wide), lambda c, j, core: (0, j))
    spec = pl.BlockSpec((rows, wide), lambda c, j, core: (2 * c + part, j))
    shape = jax.ShapeDtypeStruct(weight.shape, BF)
    return pl.pallas_call(
        update_kernel,
        grid_spec=pltpu.PrefetchScalarGridSpec(
            num_scalar_prefetch=1,
            grid=(2, across),
            in_specs=[
                pl.BlockSpec(first.shape, lambda c, j, core: (0, 0)),
                pl.BlockSpec(memory_space=pltpu.SMEM),
                mine,
                mine,
                mine,
                given,
                spec,
                spec,
                spec,
            ]
            + [pl.BlockSpec(memory_space=pl.ANY)] * len(earlier),
            out_specs=[spec, spec, spec],
            scratch_shapes=[pltpu.VMEM((first.shape[0] * STRIP, first.shape[1] * STRIP), BF)],
        ),
        out_shape=[shape, shape, shape],
        input_output_aliases={10 + k: k for k in range(len(earlier))},
        cost_estimate=pl.CostEstimate(flops=10**10, bytes_accessed=6 * MIB, transcendentals=10**6),
        name="update",
    )(core, first, mlp_out, *sums, other, weight, moment, second, *earlier)


def first_layer(mlp_in, mlp_bias):
    def split(v):
        high = lax.reduce_precision(v, 8, 7)
        middle = lax.reduce_precision(v - high, 8, 7)
        return high, middle, v - high - middle

    high, low, _ = split(mlp_in)
    bias = jnp.stack(split(mlp_bias), axis=1)
    return jnp.concatenate([high, high, low, bias], axis=1).astype(BF)


def widen(table):
    units, parts = table.shape
    shape = (units * STRIP, parts * STRIP)

    def iota(sizes, axis):
        return lax.broadcasted_iota(jnp.int32, sizes, axis)

    down = iota((shape[0], units), 0) // STRIP == iota((shape[0], units), 1)
    across = iota((parts, shape[1]), 0) == iota((parts, shape[1]), 1) // STRIP
    tall = jnp.dot(down.astype(F32).astype(BF), table, preferred_element_type=F32).astype(BF)
    wide = jnp.dot(tall, across.astype(F32).astype(BF), preferred_element_type=F32)
    return jnp.where(iota(shape, 0) % STRIP == iota(shape, 1) % STRIP, wide, 0.0).astype(BF)


def per_device(
    grad_out, route_weight, expert_ids, hidden, weight, moment, second, mlp_in, mlp_bias, mlp_out
):
    expert = lax.axis_index("expert")
    place = lax.axis_index("dp")
    core = lax.axis_index("tensor")
    groups = lax.axis_size("dp")
    cores = lax.axis_size("tensor")
    tokens = grad_out.shape[0]
    sources = hidden.shape[2]
    rows = weight.shape[1] // cores
    half = rows // 2

    near = hidden[0, 0]
    far = lax.ppermute(near, "tensor", [(0, 1), (1, 0)])

    features = grad_out.T.reshape(groups // cores, cores, rows, tokens)
    keep = lax.dynamic_index_in_dim(features, core, 1, keepdims=False)
    give = lax.dynamic_index_in_dim(features, 1 - core, 1, keepdims=False)
    slices = jnp.concatenate([keep, lax.ppermute(give, "tensor", [(0, 1), (1, 0)])], axis=0)
    shift = place + core * (groups // cores)
    ordered = [
        lax.dynamic_index_in_dim(slices, (shift + offset) % groups, 0, keepdims=False) for offset in OFFSETS
    ]

    ids = expert_ids.T.astype(BF)
    weights = route_weight.T
    weight_high = lax.reduce_precision(weights, 8, 7)
    weight_low = (weights - weight_high).astype(BF)
    table = jnp.concatenate([ids, weight_high.astype(BF), weight_low, jnp.zeros_like(ids)], axis=0)
    first = first_layer(mlp_in, mlp_bias)

    block_a = jnp.concatenate([ordered[0], ordered[1][:half], table], axis=0)
    block_b = jnp.concatenate([ordered[1][half:], ordered[2]], axis=0)
    soon = jnp.concatenate([ordered[3], ordered[4]] + [block[:half] for block in ordered[5:]], axis=0)
    late = jnp.concatenate([block[half:] for block in ordered[5:]], axis=0)
    soon, late = (lax.all_gather(block, "expert", axis=0) for block in (soon, late))
    pieces_a, pieces_b, tables, (first,) = torus_pair_gather(block_a, block_b, (first,))
    order_a, order_b = piece_sources(expert, True), piece_sources(expert, False)
    plain = jnp.arange(sources, dtype=jnp.int32)
    places = jnp.sum(jnp.where(order_a[None, :] == plain[:, None], plain[None, :], 0), axis=1)
    meta = jnp.concatenate([jnp.stack([expert, core]).astype(jnp.int32), places.astype(jnp.int32)])
    spread = spread_hidden(meta, tables, near, far)

    parts = {}

    def make(order, pieces, names):
        made = products(order, pieces, spread, [name[0] for name in names], half)
        parts.update({name[1:]: value for name, value in zip(names, made)})

    make(order_a, pieces_a, [(0, 4, 0), (1, 4, 1), (2, 3, 0)])
    make(order_b, pieces_b, [(0, 3, 1), (1, -3, 0), (2, -3, 1)])
    make(plain, (soon,), [(0, 2, 0), (1, 2, 1), (2, -2, 0), (3, -2, 1)])
    make(plain, (soon,), [(4, 1, 0), (5, -1, 0), (6, 0, 0)])
    make(plain, (late,), [(0, 1, 1), (1, -1, 1), (2, 0, 1)])

    rise = [(i, (i + 1) % groups) for i in range(groups)]
    fall = [(i, (i - 1) % groups) for i in range(groups)]
    chains = {
        (0, 1): [4, 3, 2, 1],
        (1, -1): [4, -3, -2, -1],
        (0, -1): [-3, -2, -1],
        (1, 1): [3, 2, 1],
    }
    moving = {}
    for step in range(4):
        for (part, way), chain in chains.items():
            at = step - (4 - len(chain))
            if at < 0:
                continue
            value = parts[chain[at], part]
            if at > 0:
                value = (moving[part, way].astype(F32) + value.astype(F32)).astype(BF)
            moving[part, way] = lax.ppermute(value, "dp", rise if way == 1 else fall)

    columns = hidden.shape[-1]
    outs = ()
    for part in range(2):
        moved = (moving[part, 1], moving[part, -1])
        if outs:
            moved, outs = after(moved, outs)
        sums = moved + (parts[0, part],)
        given = sum(
            lax.dynamic_slice_in_dim(v, (1 - core) * columns, columns, axis=1).astype(F32) for v in sums
        )
        other = lax.ppermute(given, "tensor", [(0, 1), (1, 0)])
        outs = update(
            core.astype(jnp.int32)[None], first, mlp_out, sums, other, weight[0], moment[0], second[0], part, outs
        )
    return tuple(out[None] for out in outs)


def solution(mesh):
    split = P("expert", "dp", "tensor")
    return jax.shard_map(
        per_device,
        mesh=mesh,
        in_specs=(
            P(("expert", "dp"), "tensor"),
            P(("expert", "dp"), None),
            P(("expert", "dp"), None),
            P("expert", "dp", None, None, "tensor"),
            split,
            split,
            split,
            P(),
            P(),
            P(),
        ),
        out_specs=(split, split, split),
        check_vma=False,
    )
```
